32 devices in a mesh: grp: 4 (over y, x), ta: 8 (over z, core).
Axes of the slice: x: 2, y: 2, z: 4, core: 2. Of those that a mesh axis runs over, the one named last changes fastest.
Arguments:
- transition: float32 [256, 256], replicated, may hold values from -1 to 1, as said below
- filtered_mean: float32 [512, 256], P(('grp', 'ta')), may hold values from -6 to 6
- filtered_cov: float32 [512, 256, 256], P(('grp', 'ta')), may hold values from -1 to 2, as said below
- pred_precision: float32 [512, 256, 256], P(('grp', 'ta')), may hold values from -1 to 2, as said below
Outputs:
- smoothed_mean: float32 [512, 256], P(('grp', 'ta'))
- smoothed_cov: float32 [512, 256, 256], P(('grp', 'ta'))
The draws below stay inside these ranges and needn't reach their ends.
Inputs may be any that keep to these rules, and one draw needn't show every extreme that they name: transition is dominated by its diagonal. Each filtered_cov at a step is symmetric with a positive diagonal. Each pred_precision at a step is symmetric with a positive diagonal.
All inputs are finite; a program needn't handle non-finite values.
Results may differ from the reference program's by a relative error of at most 0.0003.
Values sent between devices are 32-bit elements; how exact they have to be, the bound alone decides.
A program may use at most 192 MiB of HBM per device.

```python
import math
import jax
import jax.numpy as jnp
from jax import lax

STATE_DIM = 256
TIME_STEPS = 512


def rough_draw(key, shape):
    return jax.random.truncated_normal(key, -3.0, 3.0, shape, jnp.float32)


def model_streams(key):
    return jax.random.split(jax.random.fold_in(key, 7), 16)


def slow_flags(key):
    sequence_count = model_streams(key)
    share_slow = 0.5
    return jax.random.bernoulli(sequence_count[7], share_slow, (STATE_DIM,)).astype(jnp.float32)


def slow_decay(key):
    sequence_count = model_streams(key)
    return jnp.exp(jax.random.uniform(sequence_count[8], (STATE_DIM,), jnp.float32, math.log(0.1), math.log(1.0)))


def slow_rates(key):
    sequence_count = model_streams(key)
    decay_factor = slow_decay(key)
    small_perturbation = jax.random.uniform(sequence_count[9], (TIME_STEPS, STATE_DIM), jnp.float32, 0.5, 1.5)
    spike_steps = jax.random.randint(sequence_count[10], (2, STATE_DIM), 0, TIME_STEPS)
    spike_lengths = jax.random.uniform(sequence_count[11], (2, STATE_DIM), jnp.float32, 0.6, 0.8)
    time_column = jnp.arange(TIME_STEPS, dtype=jnp.int32)[:, None]
    leading_spike = jnp.where(time_column == spike_steps[0][None, :], spike_lengths[0][None, :], 1.0)
    trailing_spike = jnp.where(time_column == spike_steps[1][None, :], spike_lengths[1][None, :], 1.0)
    return jnp.exp(-decay_factor[None, :] * small_perturbation / TIME_STEPS) * leading_spike * trailing_spike


def transition_diag(key):
    sequence_count = model_streams(key)
    slow = slow_flags(key)
    fast_part = jax.random.uniform(sequence_count[0], (STATE_DIM,), jnp.float32, 0.85, 1.0)
    slow_part = jnp.exp(-jax.random.uniform(sequence_count[12], (STATE_DIM,), jnp.float32, 0.0, 1.0) / TIME_STEPS)
    return slow * slow_part + (1.0 - slow) * fast_part


def cov_diag(key):
    sequence_count = model_streams(key)
    return jnp.exp(jax.random.uniform(sequence_count[2], (TIME_STEPS, STATE_DIM), jnp.float32, math.log(0.6), math.log(1.6)))


def symmetric_off(key, spread, slow):
    identity_mat = jnp.eye(STATE_DIM, dtype=jnp.float32)
    fast_pair = (1.0 - slow)[:, None] * (1.0 - slow)[None, :]
    pair_scale = fast_pair * spread + (1.0 - fast_pair) * (0.2 / math.sqrt(TIME_STEPS))
    raw_off = rough_draw(key, (TIME_STEPS, STATE_DIM, STATE_DIM)) * (pair_scale[None, :, :] / math.sqrt(STATE_DIM))
    return (raw_off + jnp.swapaxes(raw_off, 1, 2)) * (1.0 - identity_mat)


def draw_transition(key, part):
    sequence_count = model_streams(key)
    slow = slow_flags(key)
    identity_mat = jnp.eye(STATE_DIM, dtype=jnp.float32)
    diag_part = transition_diag(key)
    row_scale = slow * jnp.sqrt(2.0 * slow_decay(key) / TIME_STEPS) + (1.0 - slow) * 0.1
    fast_columns = rough_draw(sequence_count[1], (STATE_DIM, STATE_DIM)) * (row_scale[:, None] / math.sqrt(STATE_DIM)) * (1.0 - slow)[None, :]
    slow_columns = rough_draw(sequence_count[13], (STATE_DIM, STATE_DIM)) * (0.1 / TIME_STEPS / math.sqrt(STATE_DIM)) * slow[None, :]
    return diag_part[:, None] * identity_mat + (1.0 - identity_mat) * (fast_columns + slow_columns)


def draw_filtered_cov(key, part):
    sequence_count = model_streams(key)
    slow = slow_flags(key)
    identity_mat = jnp.eye(STATE_DIM, dtype=jnp.float32)
    diag_part = cov_diag(key)
    return diag_part[:, :, None] * identity_mat + symmetric_off(sequence_count[3], 0.07, slow)


def draw_pred_precision(key, part):
    sequence_count = model_streams(key)
    slow = slow_flags(key)
    identity_mat = jnp.eye(STATE_DIM, dtype=jnp.float32)
    base_rates = jnp.exp(jax.random.uniform(sequence_count[4], (STATE_DIM,), jnp.float32, math.log(0.4), math.log(0.9)))
    fast_rates = base_rates * jax.random.uniform(sequence_count[5], (TIME_STEPS, STATE_DIM), jnp.float32, 0.85, 1.05)
    rates_all = slow[None, :] * slow_rates(key) + (1.0 - slow)[None, :] * fast_rates
    diag_part = rates_all / (transition_diag(key)[None, :] * cov_diag(key))
    return diag_part[:, :, None] * identity_mat + symmetric_off(sequence_count[6], 0.07, slow)


def shard_levels(rng, extent, pieces, least, high):
    level = 1.0
    for dim, parts in pieces:
        heights = jax.random.uniform(jax.random.fold_in(jax.random.fold_in(rng, 6), dim), (parts,), jnp.float32, least / len(pieces), high / len(pieces))
        level = level * jnp.repeat(jnp.exp(heights), extent[dim] // parts).reshape((-1,) + (1,) * (len(extent) - 1 - dim))
    return level


def scatter_about(key, shape, scale, reach, cuts=(), kind=jnp.bfloat16):
    array = jax.random.normal(key, shape, jnp.float32) * scale
    if len(cuts) > 0:
        array = shard_levels(key, shape, cuts, -0.22, 0.18) * array
    return jnp.clip(array, min=-reach, max=reach).astype(kind)


def setup_inputs(seed: int = 0) -> dict:
    arg_keys = jax.random.split(jax.random.key(seed), 5)
    return {
        "transition": draw_transition(jax.random.fold_in(arg_keys[4], 71), 0),
        "filtered_mean": scatter_about(arg_keys[1], (TIME_STEPS, STATE_DIM), 1.0, 6.0, ((0, 32),), jnp.float32),
        "filtered_cov": draw_filtered_cov(jax.random.fold_in(arg_keys[4], 71), 0),
        "pred_precision": draw_pred_precision(jax.random.fold_in(arg_keys[4], 71), 0),
    }


def reference(transition, filtered_mean, filtered_cov, pred_precision):
    highest = lax.Precision.HIGHEST
    final_index = TIME_STEPS - 1

    def advance(carried, entries):
        mean_next, cov_next = carried
        mean_now, cov_now, prec_now, position = entries
        moved_cov = jnp.dot(transition, cov_now, precision=highest, preferred_element_type=jnp.float32)
        gain_mat = jnp.dot(moved_cov.T, prec_now, precision=highest, preferred_element_type=jnp.float32)
        keep_mask = jnp.where(position < final_index, 1.0, 0.0).astype(jnp.float32)
        gain_mat = gain_mat * keep_mask
        predicted = jnp.dot(transition, mean_now, precision=highest, preferred_element_type=jnp.float32)
        offset = mean_now - jnp.dot(gain_mat, predicted, precision=highest, preferred_element_type=jnp.float32)
        leftover = cov_now - jnp.dot(gain_mat, moved_cov, precision=highest, preferred_element_type=jnp.float32)
        mean_out = jnp.dot(gain_mat, mean_next, precision=highest, preferred_element_type=jnp.float32) + offset
        inner = jnp.dot(gain_mat, cov_next, precision=highest, preferred_element_type=jnp.float32)
        cov_out = jnp.dot(inner, gain_mat.T, precision=highest, preferred_element_type=jnp.float32) + leftover
        return (mean_out, cov_out), (mean_out, cov_out)

    start = (jnp.zeros((STATE_DIM,), jnp.float32), jnp.zeros((STATE_DIM, STATE_DIM), jnp.float32))
    positions = jnp.arange(TIME_STEPS, dtype=jnp.int32)
    final_state, outputs = lax.scan(advance, start, (filtered_mean, filtered_cov, pred_precision, positions), reverse=True)
    return outputs[0], outputs[1]
```

```python
import functools
import jax
import jax.numpy as jnp
from jax import lax
from jax.experimental import pallas as pl
from jax.experimental.pallas import tpu as pltpu
from jax.sharding import PartitionSpec as P

F32 = jnp.float32
BF16 = jnp.bfloat16
MESH = pl.DeviceIdType.MESH
PAD = 16


def split(x):
    hi = x.astype(BF16)
    lo = (x - hi.astype(F32)).astype(BF16)
    return hi, lo


def left(x):
    hi, lo = split(x)
    return jnp.concatenate([hi, hi, lo], axis=1)


def right(x):
    hi, lo = split(x)
    return jnp.concatenate([hi, lo, hi], axis=0)


def right_t(x):
    hi, lo = split(x)
    return jnp.concatenate([hi, lo, hi], axis=1)


def split3(x):
    hi = x.astype(BF16)
    rest = x - hi.astype(F32)
    mid = rest.astype(BF16)
    return hi, mid, (rest - mid.astype(F32)).astype(BF16)


def left6(x):
    hi, mid, lo = split3(x)
    return jnp.concatenate([hi, hi, mid, hi, mid, lo], axis=1)


def right6(x, axis):
    hi, mid, lo = split3(x)
    return jnp.concatenate([hi, mid, hi, lo, mid, hi], axis=axis)


def left4(x):
    hi, lo = split(x)
    return jnp.concatenate([hi, hi, lo, lo], axis=1)


def right4(x, axis):
    hi, lo = split(x)
    return jnp.concatenate([hi, lo, hi, lo], axis=axis)


def mm(a3, b3):
    return lax.dot_general(a3, b3, (((1,), (0,)), ((), ())), preferred_element_type=F32)


def mm_t(a3, b3):
    return lax.dot_general(a3, b3, (((1,), (1,)), ((), ())), preferred_element_type=F32)


def wide(row):
    return jnp.broadcast_to(row[:1, :], (PAD, row.shape[1]))


def push(inner, row, e_t, cut=left):
    n = inner.shape[0]
    out = mm_t(cut(jnp.concatenate([inner, wide(row)], axis=0)), e_t)
    return out[:n], out[n:n + 1]


def compose(first, second, want_e=True):
    e1, g1, l1 = first
    e2, g2, l2 = second
    e1l = left(e1)
    inner = mm(e1l, right(l2))
    e = mm(e1l, right(e2)) if want_e else None
    l, g = push(inner, g2, right_t(e1))
    return e, g + g1, l + l1


def local_kernel(blocks, length, a_ref, m_ref, p_ref, q_ref, e_ref, l_ref, g_ref, tot_ref, acc_e, acc_l, acc_g):
    s = pl.program_id(0)
    n = a_ref.shape[0]
    last_dev = jnp.logical_and(
        lax.axis_index("grp") == lax.axis_size("grp") - 1,
        lax.axis_index("ta") == lax.axis_size("ta") - 1,
    )
    at = right6(a_ref[...], 1)
    rows = [p_ref[b, 0] for b in range(blocks)] + [wide(m_ref[b, 0]) for b in range(blocks)]
    moved = mm_t(left6(jnp.concatenate(rows, axis=0)), at)
    gains = []
    for b in range(blocks):
        gain = mm(left6(moved[b * n:(b + 1) * n]), right6(q_ref[b, 0], 0))
        if b == blocks - 1:
            gain = jnp.where(jnp.logical_and(last_dev, s == 0), jnp.zeros_like(gain), gain)
        gains.append(gain)

    def finish(b, e, inner, row):
        start = blocks * n + b * PAD
        l, g = push(inner - moved[b * n:(b + 1) * n], row - moved[start:start + 1], right4(gains[b], 1), left4)
        l = l + p_ref[b, 0]
        g = g + m_ref[b, 0]
        e_ref[b, 0] = e
        l_ref[b, 0] = l
        g_ref[b, 0] = g
        acc_e[b] = e
        acc_l[b] = l
        acc_g[b] = jnp.broadcast_to(g, (8, n))

    @pl.when(s == 0)
    def _():
        for b in range(blocks):
            finish(b, gains[b], jnp.zeros((n, n), F32), jnp.zeros((1, n), F32))

    @pl.when(s > 0)
    def _():
        for b in range(blocks):
            gl = left4(gains[b])
            e = mm(gl, right4(acc_e[b], 0))
            inner = mm(gl, right4(acc_l[b], 0))
            finish(b, e, inner, acc_g[b][:1])

    @pl.when(s == length - 1)
    def _():
        parts = [(acc_e[b], acc_g[b][:1], acc_l[b]) for b in range(blocks)]
        while len(parts) > 1:
            parts = [compose(parts[i], parts[i + 1]) for i in range(0, len(parts), 2)]
        e, g, l = parts[0]
        half = n + PAD
        tot_ref[0:n] = l
        tot_ref[n:half] = wide(g)
        tot_ref[half:half + n] = e
        tot_ref[half + n:2 * half] = jnp.zeros((PAD, n), F32)


def exchange_kernel(sizes, t_ref, o_ref, tot, exc, got, s_sem, r_sem, s2_sem, r2_sem):
    n = t_ref.shape[1]
    half = n + PAD
    grp, ta = lax.axis_index("grp"), lax.axis_index("ta")
    core = lax.rem(ta, 2)
    sib = (grp, ta + 1 - 2 * core)
    partners = []
    for name, size in sizes:
        step = 1
        while step < size:
            pos = ta if name == "ta" else grp
            bit = lax.rem(lax.div(pos, step), 2)
            other = pos + step - 2 * step * bit
            partners.append(((grp, other) if name == "ta" else (other, ta), bit))
            step *= 2
    rounds = len(partners)
    barrier = pltpu.get_barrier_semaphore()
    for dev, _ in partners:
        pl.semaphore_signal(barrier, inc=1, device_id=dev, device_id_type=MESH)
    pl.semaphore_wait(barrier, rounds)

    def copy(src, dst, a, b, dev):
        return pltpu.make_async_remote_copy(
            src_ref=src, dst_ref=dst, send_sem=a, recv_sem=b, device_id=dev, device_id_type=MESH)

    def read(ref):
        return ref[half:half + n], ref[n:n + 8][:1], ref[0:n]

    def write(ref, val):
        e, g, l = val
        ref[0:n] = l
        ref[n:half] = wide(g)
        ref[half:half + n] = e
        ref[half + n:2 * half] = jnp.zeros((PAD, n), F32)

    def pick(c, x, y):
        return tuple(jnp.where(c, i, j) for i, j in zip(x, y))

    for k, (dev, bit) in enumerate(partners):
        final = k == rounds - 1
        low = bit == 0
        src = t_ref if k == 0 else tot.at[k]
        if k == 0:
            send = copy(src, got.at[k], s_sem.at[k], r_sem.at[k], dev)
            send.start()
        else:
            size = half // 2 if final else half
            rows = pl.ds(pl.multiple_of(core * size, 8), size)
            send = copy(src.at[rows], got.at[k, rows], s_sem.at[k], r_sem.at[k], dev)
            send.start()
        if k > 1:
            old, new = exc.at[(k - 1) % 2], got.at[k - 1]
            was_low = partners[k - 1][1] == 0
            mine = read(old)
            write(exc.at[k % 2], pick(was_low, compose(mine, read(new)), mine))
        elif k == 1:
            was_low = partners[0][1] == 0
            eye = (lax.broadcasted_iota(jnp.int32, (n, n), 0) == lax.broadcasted_iota(jnp.int32, (n, n), 1)).astype(F32)
            write(exc.at[1], pick(was_low, read(got.at[0]), (eye, jnp.zeros((1, n), F32), jnp.zeros((n, n), F32))))
        send.wait()
        if k > 0:
            swap = copy(got.at[k, rows], got.at[k, rows], s2_sem.at[k], r2_sem.at[k], sib)
            swap.start()
            swap.wait()
        if not final:
            mine, theirs = read(src), read(got.at[k])
            write(tot.at[k + 1], compose(pick(low, mine, theirs), pick(low, theirs, mine)))
    mine = read(exc.at[(rounds - 1) % 2])
    ref = got.at[rounds - 1]
    later = (None, ref[n:n + 8][:1], ref[0:n])
    _, g, l = compose(mine, later, want_e=False)
    o_ref[0:n] = jnp.where(low, l, mine[2])
    o_ref[n:half] = wide(jnp.where(low, g, mine[1]))


def apply_kernel(length, c_ref, e_ref, l_ref, g_ref, m_ref, o_ref, carry):
    n = e_ref.shape[-1]

    @pl.when(pl.program_id(0) == 0)
    def _():
        carry[...] = c_ref[...]

    cov, mean = right(carry[0:n]), carry[n:n + 8][:1]
    for i in reversed(range(length)):
        e = e_ref[0, i]
        l, g = push(mm(left(e), cov), mean, right_t(e))
        l = l + l_ref[0, i]
        g = g + g_ref[0, i]
        o_ref[0, i] = l
        m_ref[0, i] = g
    carry[0:n] = l
    carry[n:n + PAD] = wide(g)


def body(transition, filtered_mean, filtered_cov, pred_precision):
    steps, n = filtered_mean.shape
    blocks = 4
    length = steps // blocks
    half = n + PAD
    mat = (blocks, length, n, n)
    vec = (blocks, length, 1, n)
    limit = 56 * 1024 * 1024
    flops = 2 * n * n * n * 3
    by_pos = lambda shape: pl.BlockSpec((blocks, 1) + shape, lambda s: (0, length - 1 - s, 0, 0))
    whole = lambda shape: pl.BlockSpec(shape, lambda s: (0,) * len(shape))
    e, l, g, total = pl.pallas_call(
        functools.partial(local_kernel, blocks, length),
        grid=(length,),
        in_specs=[whole((n, n)), by_pos((1, n)), by_pos((n, n)), by_pos((n, n))],
        out_specs=[by_pos((n, n)), by_pos((n, n)), by_pos((1, n)), whole((2 * half, n))],
        out_shape=[
            jax.ShapeDtypeStruct(mat, F32),
            jax.ShapeDtypeStruct(mat, F32),
            jax.ShapeDtypeStruct(vec, F32),
            jax.ShapeDtypeStruct((2 * half, n), F32),
        ],
        scratch_shapes=[
            pltpu.VMEM((blocks, n, n), F32),
            pltpu.VMEM((blocks, n, n), F32),
            pltpu.VMEM((blocks, 8, n), F32),
        ],
        compiler_params=pltpu.CompilerParams(vmem_limit_bytes=limit),
        cost_estimate=pl.CostEstimate(flops=80 * flops, bytes_accessed=16 * steps * n * n, transcendentals=0),
    )(transition, filtered_mean.reshape(vec), filtered_cov.reshape(mat), pred_precision.reshape(mat))

    sizes = (("ta", lax.axis_size("ta")), ("grp", lax.axis_size("grp")))
    rounds = sum(size.bit_length() - 1 for _, size in sizes)
    vmem = pl.BlockSpec(memory_space=pltpu.VMEM)
    carried = pl.pallas_call(
        functools.partial(exchange_kernel, sizes),
        in_specs=[vmem],
        out_specs=vmem,
        out_shape=jax.ShapeDtypeStruct((half, n), F32),
        scratch_shapes=[
            pltpu.VMEM((rounds, 2 * half, n), F32),
            pltpu.VMEM((2, 2 * half, n), F32),
            pltpu.VMEM((rounds, 2 * half, n), F32),
        ] + [pltpu.SemaphoreType.DMA((rounds,))] * 4,
        compiler_params=pltpu.CompilerParams(
            vmem_limit_bytes=limit, collective_id=0, has_side_effects=True),
    )(total)

    back = lambda shape: pl.BlockSpec((1, length) + shape, lambda s: (blocks - 1 - s, 0, 0, 0))
    mean, cov = pl.pallas_call(
        functools.partial(apply_kernel, length),
        grid=(blocks,),
        in_specs=[whole((half, n)), back((n, n)), back((n, n)), back((1, n))],
        out_specs=[back((1, n)), back((n, n))],
        out_shape=[jax.ShapeDtypeStruct(vec, F32), jax.ShapeDtypeStruct(mat, F32)],
        scratch_shapes=[pltpu.VMEM((half, n), F32)],
        compiler_params=pltpu.CompilerParams(vmem_limit_bytes=limit),
    )(carried, e, l, g)
    return mean.reshape(steps, n), cov.reshape(steps, n, n)


def solution(mesh):
    return jax.shard_map(
        body,
        mesh=mesh,
        in_specs=(
            P(),
            P(("grp", "ta"), None),
            P(("grp", "ta"), None, None),
            P(("grp", "ta"), None, None),
        ),
        out_specs=(P(("grp", "ta"), None), P(("grp", "ta"), None, None)),
        check_vma=False,
    )
```

```python
import functools
import jax
import jax.numpy as jnp
from jax import lax
from jax.experimental import pallas as pl
from jax.experimental.pallas import tpu as pltpu
from jax.sharding import PartitionSpec as P

F32 = jnp.float32
BF16 = jnp.bfloat16
MESH = pl.DeviceIdType.MESH
PAD = 16


def split(x):
    hi = x.astype(BF16)
    lo = (x - hi.astype(F32)).astype(BF16)
    return hi, lo


def left(x):
    hi, lo = split(x)
    return jnp.concatenate([hi, hi, lo], axis=1)


def right(x):
    hi, lo = split(x)
    return jnp.concatenate([hi, lo, hi], axis=0)


def right_t(x):
    hi, lo = split(x)
    return jnp.concatenate([hi, lo, hi], axis=1)


def split3(x):
    hi = x.astype(BF16)
    rest = x - hi.astype(F32)
    mid = rest.astype(BF16)
    return hi, mid, (rest - mid.astype(F32)).astype(BF16)


def left5(x):
    hi, lo = split(x)
    return jnp.concatenate([hi, hi, lo, lo, hi], axis=1)


def right5(x):
    hi, mid, lo = split3(x)
    return jnp.concatenate([hi, mid, hi, mid, lo], axis=0)


def left4(x):
    hi, lo = split(x)
    return jnp.concatenate([hi, hi, lo, lo], axis=1)


def right4(x, axis):
    hi, lo = split(x)
    return jnp.concatenate([hi, lo, hi, lo], axis=axis)


def mm(a3, b3):
    return lax.dot_general(a3, b3, (((1,), (0,)), ((), ())), preferred_element_type=F32)


def mm_t(a3, b3):
    return lax.dot_general(a3, b3, (((1,), (1,)), ((), ())), preferred_element_type=F32)


def wide(row):
    return jnp.broadcast_to(row[:1, :], (PAD, row.shape[1]))


def push(inner, row, e_t, cut=left):
    n = inner.shape[0]
    out = mm_t(cut(jnp.concatenate([inner, wide(row)], axis=0)), e_t)
    return out[:n], out[n:n + 1]


def compose(first, second, want_e=True):
    e1, g1, l1 = first
    e2, g2, l2 = second
    e1l = left(e1)
    inner = mm(e1l, right(l2))
    e = mm(e1l, right(e2)) if want_e else None
    l, g = push(inner, g2, right_t(e1))
    return e, g + g1, l + l1


def local_kernel(blocks, length, a_ref, m_ref, p_ref, q_ref, e_ref, l_ref, g_ref, tot_ref, acc_e, acc_l, acc_g, at):
    s = pl.program_id(0)
    n = a_ref.shape[0]
    last_dev = jnp.logical_and(
        lax.axis_index("grp") == lax.axis_size("grp") - 1,
        lax.axis_index("ta") == lax.axis_size("ta") - 1,
    )

    @pl.when(s == 0)
    def _():
        at[...] = right5(a_ref[...].T)

    spot = [pl.ds(b * length + length - 1 - s, 1) for b in range(blocks)]
    rows = [p_ref[b, 0] for b in range(blocks)] + [wide(m_ref[spot[b]]) for b in range(blocks)]
    moved = mm(left5(jnp.concatenate(rows, axis=0)), at[...])
    gains = []
    for b in range(blocks):
        gain = mm(left4(moved[b * n:(b + 1) * n]), right4(q_ref[b, 0], 0))
        if b == blocks - 1:
            gain = jnp.where(jnp.logical_and(last_dev, s == 0), jnp.zeros_like(gain), gain)
        gains.append(gain)

    def finish(b, e, inner, row):
        start = blocks * n + b * PAD
        l, g = push(inner - moved[b * n:(b + 1) * n], row - moved[start:start + 1], right4(gains[b], 1), left4)
        l = l + p_ref[b, 0]
        g = g + m_ref[spot[b]]
        e_ref[b, 0] = e
        l_ref[b, 0] = l
        g_ref[spot[b]] = g
        acc_e[b] = e
        acc_l[b] = l
        acc_g[b] = jnp.broadcast_to(g, (8, n))

    @pl.when(s == 0)
    def _():
        for b in range(blocks):
            finish(b, gains[b], jnp.zeros((n, n), F32), jnp.zeros((1, n), F32))

    @pl.when(s > 0)
    def _():
        for b in range(blocks):
            gl = left4(gains[b])
            e = mm(gl, right4(acc_e[b], 0))
            inner = mm(gl, right4(acc_l[b], 0))
            finish(b, e, inner, acc_g[b][:1])

    @pl.when(s == length - 1)
    def _():
        parts = [(acc_e[b], acc_g[b][:1], acc_l[b]) for b in range(blocks)]
        while len(parts) > 1:
            parts = [compose(parts[i], parts[i + 1]) for i in range(0, len(parts), 2)]
        e, g, l = parts[0]
        half = n + PAD
        tot_ref[0:n] = l
        tot_ref[n:half] = wide(g)
        tot_ref[half:half + n] = e
        tot_ref[half + n:2 * half] = jnp.zeros((PAD, n), F32)


def exchange_kernel(sizes, t_ref, o_ref, tot, exc, got, s_sem, r_sem, s2_sem, r2_sem, s3_sem):
    n = t_ref.shape[1]
    half = n + PAD
    grp, ta = lax.axis_index("grp"), lax.axis_index("ta")
    core = lax.rem(ta, 2)
    sib = (grp, ta + 1 - 2 * core)
    partners = []
    relay = -1
    for name, size in sizes:
        step = 1
        while step < size:
            pos = ta if name == "ta" else grp
            bit = lax.rem(lax.div(pos, step), 2)
            other = pos + step - 2 * step * bit
            if name == "ta" and step == 4:
                below = lax.rem(lax.div(pos, 2), 2)
                near = (grp, pos + 2 - 4 * below)
                edge = below != bit
                other = other + 2 - 4 * below
                relay = len(partners)
            partners.append(((grp, other) if name == "ta" else (other, ta), bit))
            step *= 2
    rounds = len(partners)
    barrier = pltpu.get_barrier_semaphore()
    for dev, _ in partners:
        pl.semaphore_signal(barrier, inc=1, device_id=dev, device_id_type=MESH)
    pl.semaphore_wait(barrier, rounds)

    def copy(src, dst, a, b, dev):
        return pltpu.make_async_remote_copy(
            src_ref=src, dst_ref=dst, send_sem=a, recv_sem=b, device_id=dev, device_id_type=MESH)

    def read(ref):
        return ref[half:half + n], ref[n:n + 8][:1], ref[0:n]

    def write(ref, val):
        e, g, l = val
        ref[0:n] = l
        ref[n:half] = wide(g)
        ref[half:half + n] = e
        ref[half + n:2 * half] = jnp.zeros((PAD, n), F32)

    def pick(c, x, y):
        return tuple(jnp.where(c, i, j) for i, j in zip(x, y))

    def extend(k):
        was_low = partners[k - 1][1] == 0
        if k == 1:
            eye = (lax.broadcasted_iota(jnp.int32, (n, n), 0) == lax.broadcasted_iota(jnp.int32, (n, n), 1)).astype(F32)
            write(exc.at[1], pick(was_low, read(got.at[0]), (eye, jnp.zeros((1, n), F32), jnp.zeros((n, n), F32))))
        else:
            mine = read(exc.at[(k - 1) % 2])
            write(exc.at[k % 2], pick(was_low, compose(mine, read(got.at[k - 1])), mine))

    def guard(k):
        return pl.when(edge) if k == relay else (lambda f: f())

    for k, (dev, bit) in enumerate(partners):
        final = k == rounds - 1
        low = bit == 0
        src = t_ref if k == 0 else tot.at[k]
        if k == 0:
            send = copy(src, got.at[k], s_sem.at[k, 0], r_sem.at[k, 0], dev)
            send.start()
            send.wait()
        else:
            size = half // 2 if final else half
            count = 2 if final else 4
            each = size // count // 8 * 8
            sends, swaps, passes = [], [], []
            for c in range(count):
                length = each if c < count - 1 else size - each * (count - 1)
                rows = pl.ds(pl.multiple_of(core * size + c * each, 8), length)
                spot = got.at[k, rows]
                sends.append(copy(src.at[rows], spot, s_sem.at[k, c], r_sem.at[k, c], dev))
                swaps.append(copy(spot, spot, s2_sem.at[k, c], r2_sem.at[k, c], sib))
                if k == relay:
                    passes.append(copy(spot, spot, s3_sem.at[c], r_sem.at[k, c], near))

            @guard(k)
            def _():
                for send in sends:
                    send.start()

            if k != relay:
                extend(k)
            for c in range(count):
                sends[c].wait_recv()
                if k == relay:
                    pl.when(edge)(passes[c].start)
                swaps[c].start()
                if k == relay and c == 1:
                    extend(k)
            for swap in swaps:
                swap.wait()

            @guard(k)
            def _():
                for send in sends:
                    send.wait_send()
                for send in passes:
                    send.wait_send()
        if not final:
            mine, theirs = read(src), read(got.at[k])
            write(tot.at[k + 1], compose(pick(low, mine, theirs), pick(low, theirs, mine)))
    mine = read(exc.at[(rounds - 1) % 2])
    ref = got.at[rounds - 1]
    later = (None, ref[n:n + 8][:1], ref[0:n])
    _, g, l = compose(mine, later, want_e=False)
    o_ref[0:n] = jnp.where(low, l, mine[2])
    o_ref[n:half] = wide(jnp.where(low, g, mine[1]))


def apply_kernel(blocks, length, c_ref, e_ref, l_ref, g_ref, m_ref, o_ref, carry):
    n = e_ref.shape[-1]

    @pl.when(pl.program_id(0) == 0)
    def _():
        carry[...] = c_ref[...]

    cov, mean = right(carry[0:n]), carry[n:n + 8][:1]
    for i in reversed(range(length)):
        e = e_ref[0, i]
        l, g = push(mm(left(e), cov), mean, right_t(e))
        l = l + l_ref[0, i]
        spot = pl.ds((blocks - 1 - pl.program_id(0)) * length + i, 1)
        g = g + g_ref[spot]
        o_ref[0, i] = l
        m_ref[spot] = g
    carry[0:n] = l
    carry[n:n + PAD] = wide(g)


def body(transition, filtered_mean, filtered_cov, pred_precision):
    steps, n = filtered_mean.shape
    blocks = 4
    length = steps // blocks
    half = n + PAD
    mat = (blocks, length, n, n)
    limit = 56 * 1024 * 1024
    flops = 2 * n * n * n * 3
    by_pos = lambda shape: pl.BlockSpec((blocks, 1) + shape, lambda s: (0, length - 1 - s, 0, 0))
    whole = lambda shape: pl.BlockSpec(shape, lambda s: (0,) * len(shape))
    e, l, g, total = pl.pallas_call(
        functools.partial(local_kernel, blocks, length),
        grid=(length,),
        in_specs=[whole((n, n)), whole((steps, n)), by_pos((n, n)), by_pos((n, n))],
        out_specs=[by_pos((n, n)), by_pos((n, n)), whole((steps, n)), whole((2 * half, n))],
        out_shape=[
            jax.ShapeDtypeStruct(mat, F32),
            jax.ShapeDtypeStruct(mat, F32),
            jax.ShapeDtypeStruct((steps, n), F32),
            jax.ShapeDtypeStruct((2 * half, n), F32),
        ],
        scratch_shapes=[
            pltpu.VMEM((blocks, n, n), F32),
            pltpu.VMEM((blocks, n, n), F32),
            pltpu.VMEM((blocks, 8, n), F32),
            pltpu.VMEM((5 * n, n), BF16),
        ],
        compiler_params=pltpu.CompilerParams(vmem_limit_bytes=limit),
        cost_estimate=pl.CostEstimate(flops=80 * flops, bytes_accessed=16 * steps * n * n, transcendentals=0),
    )(transition, filtered_mean, filtered_cov.reshape(mat), pred_precision.reshape(mat))

    sizes = (("ta", lax.axis_size("ta")), ("grp", lax.axis_size("grp")))
    rounds = sum(size.bit_length() - 1 for _, size in sizes)
    vmem = pl.BlockSpec(memory_space=pltpu.VMEM)
    carried = pl.pallas_call(
        functools.partial(exchange_kernel, sizes),
        in_specs=[vmem],
        out_specs=vmem,
        out_shape=jax.ShapeDtypeStruct((half, n), F32),
        scratch_shapes=[
            pltpu.VMEM((rounds, 2 * half, n), F32),
            pltpu.VMEM((2, 2 * half, n), F32),
            pltpu.VMEM((rounds, 2 * half, n), F32),
        ] + [pltpu.SemaphoreType.DMA((rounds, 4))] * 4 + [pltpu.SemaphoreType.DMA((4,))],
        compiler_params=pltpu.CompilerParams(
            vmem_limit_bytes=limit, collective_id=0, has_side_effects=True),
    )(total)

    back = lambda shape: pl.BlockSpec((1, length) + shape, lambda s: (blocks - 1 - s, 0, 0, 0))
    mean, cov = pl.pallas_call(
        functools.partial(apply_kernel, blocks, length),
        grid=(blocks,),
        in_specs=[whole((half, n)), back((n, n)), back((n, n)), whole((steps, n))],
        out_specs=[whole((steps, n)), back((n, n))],
        out_shape=[jax.ShapeDtypeStruct((steps, n), F32), jax.ShapeDtypeStruct(mat, F32)],
        scratch_shapes=[pltpu.VMEM((half, n), F32)],
        compiler_params=pltpu.CompilerParams(vmem_limit_bytes=limit),
    )(carried, e, l, g)
    return mean, cov.reshape(steps, n, n)


def solution(mesh):
    return jax.shard_map(
        body,
        mesh=mesh,
        in_specs=(
            P(),
            P(("grp", "ta"), None),
            P(("grp", "ta"), None, None),
            P(("grp", "ta"), None, None),
        ),
        out_specs=(P(("grp", "ta"), None), P(("grp", "ta"), None, None)),
        check_vma=False,
    )
```

```python
import functools
import jax
import jax.numpy as jnp
from jax import lax
from jax.experimental import pallas as pl
from jax.experimental.pallas import tpu as pltpu
from jax.sharding import PartitionSpec as P

F32 = jnp.float32
BF16 = jnp.bfloat16
MESH = pl.DeviceIdType.MESH
PAD = 16


def split(x):
    hi = x.astype(BF16)
    lo = (x - hi.astype(F32)).astype(BF16)
    return hi, lo


def left(x):
    hi, lo = split(x)
    return jnp.concatenate([hi, hi, lo], axis=1)


def right(x):
    hi, lo = split(x)
    return jnp.concatenate([hi, lo, hi], axis=0)


def right_t(x):
    hi, lo = split(x)
    return jnp.concatenate([hi, lo, hi], axis=1)


def unit(n):
    return (lax.broadcasted_iota(jnp.int32, (n, n), 0) == lax.broadcasted_iota(jnp.int32, (n, n), 1)).astype(F32)


def mm(a3, b3):
    return lax.dot_general(a3, b3, (((1,), (0,)), ((), ())), preferred_element_type=F32)


def mm_t(a3, b3):
    return lax.dot_general(a3, b3, (((1,), (1,)), ((), ())), preferred_element_type=F32)


def wide(row):
    return jnp.broadcast_to(row[:1, :], (PAD, row.shape[1]))


def push(inner, row, e_t, near=False):
    n = inner.shape[0]
    both = jnp.concatenate([inner, wide(row)], axis=0)
    out = mm_t(left(both), e_t)
    if near:
        out = both + out
    return out[:n], out[n:n + 1]


def compose(first, second, want_e=True):
    e1, g1, l1 = first
    e2, g2, l2 = second
    e1l = left(e1)
    inner = mm(e1l, right(l2))
    e = mm(e1l, right(e2)) if want_e else None
    l, g = push(inner, g2, right_t(e1))
    return e, g + g1, l + l1


def local_kernel(blocks, length, a_ref, m_ref, p_ref, q_ref, e_ref, l_ref, g_ref, tot_ref, acc_e, acc_l, acc_g, at):
    s = pl.program_id(0)
    n = a_ref.shape[0]
    last_dev = jnp.logical_and(
        lax.axis_index("grp") == lax.axis_size("grp") - 1,
        lax.axis_index("ta") == lax.axis_size("ta") - 1,
    )

    @pl.when(s == 0)
    def _():
        at[...] = right((a_ref[...] - unit(n)).T)

    spot = [pl.ds(b * length + length - 1 - s, 1) for b in range(blocks)]
    rows = [p_ref[b, 0] for b in range(blocks)] + [wide(m_ref[spot[b]]) for b in range(blocks)]
    rows = jnp.concatenate(rows, axis=0)
    moved = rows + mm(left(rows), at[...])
    gains = []
    eye = unit(n)
    for b in range(blocks):
        gain = mm(left(moved[b * n:(b + 1) * n]), right(q_ref[b, 0]))
        if b == blocks - 1:
            gain = jnp.where(jnp.logical_and(last_dev, s == 0), jnp.zeros_like(gain), gain)
        gains.append(gain)

    def finish(b, e, inner, row):
        start = blocks * n + b * PAD
        l, g = push(inner - moved[b * n:(b + 1) * n], row - moved[start:start + 1], right_t(gains[b] - eye), True)
        l = l + p_ref[b, 0]
        g = g + m_ref[spot[b]]
        e_ref[b, 0] = e
        l_ref[b, 0] = l
        g_ref[spot[b]] = g
        acc_e[b] = e
        acc_l[b] = l
        acc_g[b] = jnp.broadcast_to(g, (8, n))

    @pl.when(s == 0)
    def _():
        for b in range(blocks):
            finish(b, gains[b], jnp.zeros((n, n), F32), jnp.zeros((1, n), F32))

    @pl.when(s > 0)
    def _():
        for b in range(blocks):
            gl = left(gains[b] - eye)
            e = acc_e[b] + mm(gl, right(acc_e[b]))
            inner = acc_l[b] + mm(gl, right(acc_l[b]))
            finish(b, e, inner, acc_g[b][:1])

    @pl.when(s == length - 1)
    def _():
        parts = [(acc_e[b], acc_g[b][:1], acc_l[b]) for b in range(blocks)]
        while len(parts) > 1:
            parts = [compose(parts[i], parts[i + 1]) for i in range(0, len(parts), 2)]
        e, g, l = parts[0]
        half = n + PAD
        tot_ref[0:n] = l
        tot_ref[n:half] = wide(g)
        tot_ref[half:half + n] = e
        tot_ref[half + n:2 * half] = jnp.zeros((PAD, n), F32)


def exchange_kernel(sizes, t_ref, o_ref, tot, exc, got, s_sem, r_sem, s2_sem, r2_sem, s3_sem):
    n = t_ref.shape[1]
    half = n + PAD
    grp, ta = lax.axis_index("grp"), lax.axis_index("ta")
    core = lax.rem(ta, 2)
    sib = (grp, ta + 1 - 2 * core)
    partners = []
    relay = -1
    for name, size in sizes:
        step = 1
        while step < size:
            pos = ta if name == "ta" else grp
            bit = lax.rem(lax.div(pos, step), 2)
            other = pos + step - 2 * step * bit
            if name == "ta" and step == 4:
                below = lax.rem(lax.div(pos, 2), 2)
                near = (grp, pos + 2 - 4 * below)
                edge = below != bit
                other = other + 2 - 4 * below
                relay = len(partners)
            partners.append(((grp, other) if name == "ta" else (other, ta), bit))
            step *= 2
    rounds = len(partners)
    barrier = pltpu.get_barrier_semaphore()
    for dev, _ in partners:
        pl.semaphore_signal(barrier, inc=1, device_id=dev, device_id_type=MESH)
    pl.semaphore_wait(barrier, rounds)

    def copy(src, dst, a, b, dev):
        return pltpu.make_async_remote_copy(
            src_ref=src, dst_ref=dst, send_sem=a, recv_sem=b, device_id=dev, device_id_type=MESH)

    def read(ref):
        return ref[half:half + n], ref[n:n + 8][:1], ref[0:n]

    def write(ref, val):
        e, g, l = val
        ref[0:n] = l
        ref[n:half] = wide(g)
        ref[half:half + n] = e
        ref[half + n:2 * half] = jnp.zeros((PAD, n), F32)

    def pick(c, x, y):
        return tuple(jnp.where(c, i, j) for i, j in zip(x, y))

    def extend(k):
        was_low = partners[k - 1][1] == 0
        if k == 1:
            eye = unit(n)
            write(exc.at[1], pick(was_low, read(got.at[0]), (eye, jnp.zeros((1, n), F32), jnp.zeros((n, n), F32))))
        else:
            mine = read(exc.at[(k - 1) % 2])
            write(exc.at[k % 2], pick(was_low, compose(mine, read(got.at[k - 1])), mine))

    def guard(k):
        return pl.when(edge) if k == relay else (lambda f: f())

    for k, (dev, bit) in enumerate(partners):
        final = k == rounds - 1
        low = bit == 0
        src = t_ref if k == 0 else tot.at[k]
        if k == 0:
            send = copy(src, got.at[k], s_sem.at[k, 0], r_sem.at[k, 0], dev)
            send.start()
            send.wait()
        else:
            size = half // 2 if final else half
            count = 2 if final else 4
            each = size // count // 8 * 8
            sends, swaps, passes = [], [], []
            for c in range(count):
                length = each if c < count - 1 else size - each * (count - 1)
                rows = pl.ds(pl.multiple_of(core * size + c * each, 8), length)
                spot = got.at[k, rows]
                sends.append(copy(src.at[rows], spot, s_sem.at[k, c], r_sem.at[k, c], dev))
                swaps.append(copy(spot, spot, s2_sem.at[k, c], r2_sem.at[k, c], sib))
                if k == relay:
                    passes.append(copy(spot, spot, s3_sem.at[c], r_sem.at[k, c], near))

            @guard(k)
            def _():
                for send in sends:
                    send.start()

            if k != relay:
                extend(k)
            for c in range(count):
                sends[c].wait_recv()
                if k == relay:
                    pl.when(edge)(passes[c].start)
                swaps[c].start()
                if k == relay and c == 1:
                    extend(k)
            for swap in swaps:
                swap.wait()

            @guard(k)
            def _():
                for send in sends:
                    send.wait_send()
                for send in passes:
                    send.wait_send()
        if not final:
            mine, theirs = read(src), read(got.at[k])
            write(tot.at[k + 1], compose(pick(low, mine, theirs), pick(low, theirs, mine)))
    mine = read(exc.at[(rounds - 1) % 2])
    ref = got.at[rounds - 1]
    later = (None, ref[n:n + 8][:1], ref[0:n])
    _, g, l = compose(mine, later, want_e=False)
    o_ref[0:n] = jnp.where(low, l, mine[2])
    o_ref[n:half] = wide(jnp.where(low, g, mine[1]))


def apply_kernel(blocks, length, c_ref, e_ref, l_ref, g_ref, m_ref, o_ref, carry):
    n = e_ref.shape[-1]

    @pl.when(pl.program_id(0) == 0)
    def _():
        carry[...] = c_ref[...]

    cov, mean = right(carry[0:n]), carry[n:n + 8][:1]
    for i in reversed(range(length)):
        e = e_ref[0, i]
        l, g = push(mm(left(e), cov), mean, right_t(e))
        l = l + l_ref[0, i]
        spot = pl.ds((blocks - 1 - pl.program_id(0)) * length + i, 1)
        g = g + g_ref[spot]
        o_ref[0, i] = l
        m_ref[spot] = g
    carry[0:n] = l
    carry[n:n + PAD] = wide(g)


def body(transition, filtered_mean, filtered_cov, pred_precision):
    steps, n = filtered_mean.shape
    blocks = 4
    length = steps // blocks
    half = n + PAD
    mat = (blocks, length, n, n)
    limit = 56 * 1024 * 1024
    flops = 2 * n * n * n * 3
    by_pos = lambda shape: pl.BlockSpec((blocks, 1) + shape, lambda s: (0, length - 1 - s, 0, 0))
    whole = lambda shape: pl.BlockSpec(shape, lambda s: (0,) * len(shape))
    e, l, g, total = pl.pallas_call(
        functools.partial(local_kernel, blocks, length),
        grid=(length,),
        in_specs=[whole((n, n)), whole((steps, n)), by_pos((n, n)), by_pos((n, n))],
        out_specs=[by_pos((n, n)), by_pos((n, n)), whole((steps, n)), whole((2 * half, n))],
        out_shape=[
            jax.ShapeDtypeStruct(mat, F32),
            jax.ShapeDtypeStruct(mat, F32),
            jax.ShapeDtypeStruct((steps, n), F32),
            jax.ShapeDtypeStruct((2 * half, n), F32),
        ],
        scratch_shapes=[
            pltpu.VMEM((blocks, n, n), F32),
            pltpu.VMEM((blocks, n, n), F32),
            pltpu.VMEM((blocks, 8, n), F32),
            pltpu.VMEM((3 * n, n), BF16),
        ],
        compiler_params=pltpu.CompilerParams(vmem_limit_bytes=limit),
        cost_estimate=pl.CostEstimate(flops=80 * flops, bytes_accessed=16 * steps * n * n, transcendentals=0),
    )(transition, filtered_mean, filtered_cov.reshape(mat), pred_precision.reshape(mat))

    sizes = (("ta", lax.axis_size("ta")), ("grp", lax.axis_size("grp")))
    rounds = sum(size.bit_length() - 1 for _, size in sizes)
    vmem = pl.BlockSpec(memory_space=pltpu.VMEM)
    carried = pl.pallas_call(
        functools.partial(exchange_kernel, sizes),
        in_specs=[vmem],
        out_specs=vmem,
        out_shape=jax.ShapeDtypeStruct((half, n), F32),
        scratch_shapes=[
            pltpu.VMEM((rounds, 2 * half, n), F32),
            pltpu.VMEM((2, 2 * half, n), F32),
            pltpu.VMEM((rounds, 2 * half, n), F32),
        ] + [pltpu.SemaphoreType.DMA((rounds, 4))] * 4 + [pltpu.SemaphoreType.DMA((4,))],
        compiler_params=pltpu.CompilerParams(
            vmem_limit_bytes=limit, collective_id=0, has_side_effects=True),
    )(total)

    back = lambda shape: pl.BlockSpec((1, length) + shape, lambda s: (blocks - 1 - s, 0, 0, 0))
    mean, cov = pl.pallas_call(
        functools.partial(apply_kernel, blocks, length),
        grid=(blocks,),
        in_specs=[whole((half, n)), back((n, n)), back((n, n)), whole((steps, n))],
        out_specs=[whole((steps, n)), back((n, n))],
        out_shape=[jax.ShapeDtypeStruct((steps, n), F32), jax.ShapeDtypeStruct(mat, F32)],
        scratch_shapes=[pltpu.VMEM((half, n), F32)],
        compiler_params=pltpu.CompilerParams(vmem_limit_bytes=limit),
    )(carried, e, l, g)
    return mean, cov.reshape(steps, n, n)


def solution(mesh):
    return jax.shard_map(
        body,
        mesh=mesh,
        in_specs=(
            P(),
            P(("grp", "ta"), None),
            P(("grp", "ta"), None, None),
            P(("grp", "ta"), None, None),
        ),
        out_specs=(P(("grp", "ta"), None), P(("grp", "ta"), None, None)),
        check_vma=False,
    )
```

```python
import functools
import jax
import jax.numpy as jnp
from jax import lax
from jax.experimental import pallas as pl
from jax.experimental.pallas import tpu as pltpu
from jax.sharding import PartitionSpec as P

F32 = jnp.float32
BF16 = jnp.bfloat16
MESH = pl.DeviceIdType.MESH
PAD = 16


def split(x):
    hi = x.astype(BF16)
    lo = (x - hi.astype(F32)).astype(BF16)
    return hi, lo


def left(x):
    hi, lo = split(x)
    return jnp.concatenate([hi, hi, lo], axis=1)


def right(x):
    hi, lo = split(x)
    return jnp.concatenate([hi, lo, hi], axis=0)


def right_t(x):
    hi, lo = split(x)
    return jnp.concatenate([hi, lo, hi], axis=1)


def unit(n):
    return (lax.broadcasted_iota(jnp.int32, (n, n), 0) == lax.broadcasted_iota(jnp.int32, (n, n), 1)).astype(F32)


def mm(a3, b3):
    return lax.dot_general(a3, b3, (((1,), (0,)), ((), ())), preferred_element_type=F32)


def mm_t(a3, b3):
    return lax.dot_general(a3, b3, (((1,), (1,)), ((), ())), preferred_element_type=F32)


def wide(row):
    return jnp.broadcast_to(row[:1, :], (PAD, row.shape[1]))


def push(inner, row, e_t, near=False):
    n = inner.shape[0]
    both = jnp.concatenate([inner, wide(row)], axis=0)
    out = mm_t(left(both), e_t)
    if near:
        out = both + out
    return out[:n], out[n:n + 1]


def compose(first, second, want_e=True):
    e1, g1, l1 = first
    e2, g2, l2 = second
    e1l = left(e1)
    inner = mm(e1l, right(l2))
    e = mm(e1l, right(e2)) if want_e else None
    l, g = push(inner, g2, right_t(e1))
    return e, g + g1, l + l1


def layout(n):
    tri = n // 2 + n // 4
    return tri, tri + PAD, tri + PAD + n


def load(ref, want_e=True):
    n = ref.shape[-1]
    h, (tri, start, full) = n // 2, layout(n)
    top, low = ref[0:h], ref[h:tri]
    low = jnp.concatenate([low[:, :h], low[:, h:]], axis=0)
    low = jnp.concatenate([top[:, h:].T, low], axis=1)
    return ref[start:full] if want_e else None, ref[tri:tri + 8][:1], jnp.concatenate([top, low], axis=0)


def store(ref, val):
    e, g, l = val
    n = ref.shape[-1]
    h, q, (tri, start, full) = n // 2, n // 4, layout(n)
    ref[0:h] = l[:h]
    ref[h:tri] = jnp.concatenate([l[h:h + q, h:], l[h + q:, h:]], axis=1)
    ref[tri:start] = wide(g)
    ref[start:full] = e


def local_kernel(blocks, length, a_ref, m_ref, p_ref, q_ref, e_ref, l_ref, g_ref, tot_ref, acc_e, acc_l, acc_g, at):
    s = pl.program_id(0)
    n = a_ref.shape[0]
    last_dev = jnp.logical_and(
        lax.axis_index("grp") == lax.axis_size("grp") - 1,
        lax.axis_index("ta") == lax.axis_size("ta") - 1,
    )

    @pl.when(s == 0)
    def _():
        at[...] = right((a_ref[...] - unit(n)).T)

    spot = [pl.ds(b * length + length - 1 - s, 1) for b in range(blocks)]
    rows = [p_ref[b, 0] for b in range(blocks)] + [wide(m_ref[spot[b]]) for b in range(blocks)]
    rows = jnp.concatenate(rows, axis=0)
    moved = rows + mm(left(rows), at[...])
    gains = []
    eye = unit(n)
    for b in range(blocks):
        gain = mm(left(moved[b * n:(b + 1) * n]), right(q_ref[b, 0]))
        if b == blocks - 1:
            gain = jnp.where(jnp.logical_and(last_dev, s == 0), jnp.zeros_like(gain), gain)
        gains.append(gain)

    def finish(b, e, inner, row):
        start = blocks * n + b * PAD
        l, g = push(inner - moved[b * n:(b + 1) * n], row - moved[start:start + 1], right_t(gains[b] - eye), True)
        l = l + p_ref[b, 0]
        g = g + m_ref[spot[b]]
        e_ref[b, 0] = e
        l_ref[b, 0] = l
        g_ref[spot[b]] = g
        acc_e[b] = e
        acc_l[b] = l
        acc_g[b] = jnp.broadcast_to(g, (8, n))

    @pl.when(s == 0)
    def _():
        for b in range(blocks):
            finish(b, gains[b], jnp.zeros((n, n), F32), jnp.zeros((1, n), F32))

    @pl.when(s > 0)
    def _():
        for b in range(blocks):
            gl = left(gains[b] - eye)
            e = acc_e[b] + mm(gl, right(acc_e[b]))
            inner = acc_l[b] + mm(gl, right(acc_l[b]))
            finish(b, e, inner, acc_g[b][:1])

    @pl.when(s == length - 1)
    def _():
        parts = [(acc_e[b], acc_g[b][:1], acc_l[b]) for b in range(blocks)]
        while len(parts) > 1:
            parts = [compose(parts[i], parts[i + 1]) for i in range(0, len(parts), 2)]
        store(tot_ref, parts[0])


def exchange_kernel(sizes, t_ref, o_ref, tot, exc, got, s_sem, r_sem, s2_sem, r2_sem, s3_sem):
    n = t_ref.shape[1]
    tri, start, full = layout(n)
    grp, ta = lax.axis_index("grp"), lax.axis_index("ta")
    core = lax.rem(ta, 2)
    sib = (grp, ta + 1 - 2 * core)
    partners = []
    relay = -1
    for name, size in sizes:
        step = 1
        while step < size:
            pos = ta if name == "ta" else grp
            bit = lax.rem(lax.div(pos, step), 2)
            other = pos + step - 2 * step * bit
            if name == "ta" and step == 4:
                below = lax.rem(lax.div(pos, 2), 2)
                near = (grp, pos + 2 - 4 * below)
                edge = below != bit
                other = other + 2 - 4 * below
                relay = len(partners)
            partners.append(((grp, other) if name == "ta" else (other, ta), bit))
            step *= 2
    rounds = len(partners)
    barrier = pltpu.get_barrier_semaphore()
    for dev, _ in partners:
        pl.semaphore_signal(barrier, inc=1, device_id=dev, device_id_type=MESH)
    pl.semaphore_wait(barrier, rounds)

    def copy(src, dst, a, b, dev):
        return pltpu.make_async_remote_copy(
            src_ref=src, dst_ref=dst, send_sem=a, recv_sem=b, device_id=dev, device_id_type=MESH)

    def pick(c, x, y):
        return tuple(jnp.where(c, i, j) for i, j in zip(x, y))

    def extend(k):
        was_low = partners[k - 1][1] == 0
        if k == 1:
            eye = unit(n)
            store(exc.at[1], pick(was_low, load(got.at[0]), (eye, jnp.zeros((1, n), F32), jnp.zeros((n, n), F32))))
        else:
            mine = load(exc.at[(k - 1) % 2])
            store(exc.at[k % 2], pick(was_low, compose(mine, load(got.at[k - 1])), mine))

    def guard(k):
        return pl.when(edge) if k == relay else (lambda f: f())

    for k, (dev, bit) in enumerate(partners):
        final = k == rounds - 1
        low = bit == 0
        src = t_ref if k == 0 else tot.at[k]
        if k == 0:
            send = copy(src, got.at[k], s_sem.at[k, 0], r_sem.at[k, 0], dev)
            send.start()
            send.wait()
        else:
            size = (start if final else full) // 2
            count = 2 if final else 4
            each = size // count // 8 * 8
            sends, swaps, passes = [], [], []
            for c in range(count):
                length = each if c < count - 1 else size - each * (count - 1)
                rows = pl.ds(pl.multiple_of(core * size + c * each, 8), length)
                spot = got.at[k, rows]
                sends.append(copy(src.at[rows], spot, s_sem.at[k, c], r_sem.at[k, c], dev))
                swaps.append(copy(spot, spot, s2_sem.at[k, c], r2_sem.at[k, c], sib))
                if k == relay:
                    passes.append(copy(spot, spot, s3_sem.at[c], r_sem.at[k, c], near))

            @guard(k)
            def _():
                for send in sends:
                    send.start()

            if k != relay:
                extend(k)
            for c in range(count):
                sends[c].wait_recv()
                if k == relay:
                    pl.when(edge)(passes[c].start)
                swaps[c].start()
                if k == relay and c == 1:
                    extend(k)
            for swap in swaps:
                swap.wait()

            @guard(k)
            def _():
                for send in sends:
                    send.wait_send()
                for send in passes:
                    send.wait_send()
        if not final:
            mine, theirs = load(src), load(got.at[k])
            store(tot.at[k + 1], compose(pick(low, mine, theirs), pick(low, theirs, mine)))
    mine = load(exc.at[(rounds - 1) % 2])
    _, g, l = compose(mine, load(got.at[rounds - 1], False), want_e=False)
    o_ref[0:n] = jnp.where(low, l, mine[2])
    o_ref[n:n + PAD] = wide(jnp.where(low, g, mine[1]))


def apply_kernel(blocks, length, c_ref, e_ref, l_ref, g_ref, m_ref, o_ref, carry):
    n = e_ref.shape[-1]

    @pl.when(pl.program_id(0) == 0)
    def _():
        carry[...] = c_ref[...]

    cov, mean = right(carry[0:n]), carry[n:n + 8][:1]
    for i in reversed(range(length)):
        e = e_ref[0, i]
        l, g = push(mm(left(e), cov), mean, right_t(e))
        l = l + l_ref[0, i]
        spot = pl.ds((blocks - 1 - pl.program_id(0)) * length + i, 1)
        g = g + g_ref[spot]
        o_ref[0, i] = l
        m_ref[spot] = g
    carry[0:n] = l
    carry[n:n + PAD] = wide(g)


def body(transition, filtered_mean, filtered_cov, pred_precision):
    steps, n = filtered_mean.shape
    blocks = 4
    length = steps // blocks
    half = n + PAD
    mat = (blocks, length, n, n)
    limit = 56 * 1024 * 1024
    flops = 2 * n * n * n * 3
    by_pos = lambda shape: pl.BlockSpec((blocks, 1) + shape, lambda s: (0, length - 1 - s, 0, 0))
    whole = lambda shape: pl.BlockSpec(shape, lambda s: (0,) * len(shape))
    e, l, g, total = pl.pallas_call(
        functools.partial(local_kernel, blocks, length),
        grid=(length,),
        in_specs=[whole((n, n)), whole((steps, n)), by_pos((n, n)), by_pos((n, n))],
        out_specs=[by_pos((n, n)), by_pos((n, n)), whole((steps, n)), whole((layout(n)[2], n))],
        out_shape=[
            jax.ShapeDtypeStruct(mat, F32),
            jax.ShapeDtypeStruct(mat, F32),
            jax.ShapeDtypeStruct((steps, n), F32),
            jax.ShapeDtypeStruct((layout(n)[2], n), F32),
        ],
        scratch_shapes=[
            pltpu.VMEM((blocks, n, n), F32),
            pltpu.VMEM((blocks, n, n), F32),
            pltpu.VMEM((blocks, 8, n), F32),
            pltpu.VMEM((3 * n, n), BF16),
        ],
        compiler_params=pltpu.CompilerParams(vmem_limit_bytes=limit),
        cost_estimate=pl.CostEstimate(flops=80 * flops, bytes_accessed=16 * steps * n * n, transcendentals=0),
    )(transition, filtered_mean, filtered_cov.reshape(mat), pred_precision.reshape(mat))

    sizes = (("ta", lax.axis_size("ta")), ("grp", lax.axis_size("grp")))
    rounds = sum(size.bit_length() - 1 for _, size in sizes)
    vmem = pl.BlockSpec(memory_space=pltpu.VMEM)
    carried = pl.pallas_call(
        functools.partial(exchange_kernel, sizes),
        in_specs=[vmem],
        out_specs=vmem,
        out_shape=jax.ShapeDtypeStruct((half, n), F32),
        scratch_shapes=[
            pltpu.VMEM((rounds, layout(n)[2], n), F32),
            pltpu.VMEM((2, layout(n)[2], n), F32),
            pltpu.VMEM((rounds, layout(n)[2], n), F32),
        ] + [pltpu.SemaphoreType.DMA((rounds, 4))] * 4 + [pltpu.SemaphoreType.DMA((4,))],
        compiler_params=pltpu.CompilerParams(
            vmem_limit_bytes=limit, collective_id=0, has_side_effects=True),
    )(total)

    back = lambda shape: pl.BlockSpec((1, length) + shape, lambda s: (blocks - 1 - s, 0, 0, 0))
    mean, cov = pl.pallas_call(
        functools.partial(apply_kernel, blocks, length),
        grid=(blocks,),
        in_specs=[whole((half, n)), back((n, n)), back((n, n)), whole((steps, n))],
        out_specs=[whole((steps, n)), back((n, n))],
        out_shape=[jax.ShapeDtypeStruct((steps, n), F32), jax.ShapeDtypeStruct(mat, F32)],
        scratch_shapes=[pltpu.VMEM((half, n), F32)],
        compiler_params=pltpu.CompilerParams(vmem_limit_bytes=limit),
    )(carried, e, l, g)
    return mean, cov.reshape(steps, n, n)


def solution(mesh):
    return jax.shard_map(
        body,
        mesh=mesh,
        in_specs=(
            P(),
            P(("grp", "ta"), None),
            P(("grp", "ta"), None, None),
            P(("grp", "ta"), None, None),
        ),
        out_specs=(P(("grp", "ta"), None), P(("grp", "ta"), None, None)),
        check_vma=False,
    )
```

```python
import functools
import jax
import jax.numpy as jnp
from jax import lax
from jax.experimental import pallas as pl
from jax.experimental.pallas import tpu as pltpu
from jax.sharding import PartitionSpec as P

F32 = jnp.float32
BF16 = jnp.bfloat16
MESH = pl.DeviceIdType.MESH
PAD = 16


def split(x):
    hi = x.astype(BF16)
    lo = (x - hi.astype(F32)).astype(BF16)
    return hi, lo


def left(x):
    hi, lo = split(x)
    return jnp.concatenate([hi, hi, lo], axis=1)


def right(x):
    hi, lo = split(x)
    return jnp.concatenate([hi, lo, hi], axis=0)


def right_t(x):
    hi, lo = split(x)
    return jnp.concatenate([hi, lo, hi], axis=1)


def unit(n):
    return (lax.broadcasted_iota(jnp.int32, (n, n), 0) == lax.broadcasted_iota(jnp.int32, (n, n), 1)).astype(F32)


def mm(a3, b3):
    return lax.dot_general(a3, b3, (((1,), (0,)), ((), ())), preferred_element_type=F32)


def mm_t(a3, b3):
    return lax.dot_general(a3, b3, (((1,), (1,)), ((), ())), preferred_element_type=F32)


def wide(row):
    return jnp.broadcast_to(row[:1, :], (PAD, row.shape[1]))


def push(inner, row, e_t, near=False):
    n = inner.shape[0]
    both = jnp.concatenate([inner, wide(row)], axis=0)
    out = mm_t(left(both), e_t)
    if near:
        out = both + out
    return out[:n], out[n:n + 1]


def compose(first, second, want_e=True):
    e1, g1, l1 = first
    e2, g2, l2 = second
    e1l = left(e1)
    inner = mm(e1l, right(l2))
    e = mm(e1l, right(e2)) if want_e else None
    l, g = push(inner, g2, right_t(e1))
    return e, g + g1, l + l1


def layout(n):
    tri = n // 2 + n // 4
    return tri, tri + PAD, tri + PAD + n


def load(ref, want_e=True):
    n = ref.shape[-1]
    h, (tri, start, full) = n // 2, layout(n)
    top, low = ref[0:h], ref[h:tri]
    low = jnp.concatenate([low[:, :h], low[:, h:]], axis=0)
    low = jnp.concatenate([top[:, h:].T, low], axis=1)
    return ref[start:full] if want_e else None, ref[tri:tri + 8][:1], jnp.concatenate([top, low], axis=0)


def store(ref, val):
    e, g, l = val
    n = ref.shape[-1]
    h, q, (tri, start, full) = n // 2, n // 4, layout(n)
    ref[0:h] = l[:h]
    ref[h:tri] = jnp.concatenate([l[h:h + q, h:], l[h + q:, h:]], axis=1)
    ref[tri:start] = wide(g)
    ref[start:full] = e


def local_kernel(blocks, length, a_ref, m_ref, p_ref, q_ref, e_ref, l_ref, g_ref, tot_ref, acc_e, acc_l, acc_g, at):
    s = pl.program_id(0)
    n = a_ref.shape[0]
    last_dev = jnp.logical_and(
        lax.axis_index("grp") == lax.axis_size("grp") - 1,
        lax.axis_index("ta") == lax.axis_size("ta") - 1,
    )

    @pl.when(s == 0)
    def _():
        at[...] = right((a_ref[...] - unit(n)).T)

    spot = [pl.ds(b * length + length - 1 - s, 1) for b in range(blocks)]
    rows = [p_ref[b, 0] for b in range(blocks)] + [wide(m_ref[spot[b]]) for b in range(blocks)]
    rows = jnp.concatenate(rows, axis=0)
    moved = rows + mm(left(rows), at[...])
    gains = []
    eye = unit(n)
    for b in range(blocks):
        gain = mm(left(moved[b * n:(b + 1) * n]), right(q_ref[b, 0]))
        if b == blocks - 1:
            gain = jnp.where(jnp.logical_and(last_dev, s == 0), jnp.zeros_like(gain), gain)
        gains.append(gain)

    def finish(b, e, inner, row):
        start = blocks * n + b * PAD
        l, g = push(inner - moved[b * n:(b + 1) * n], row - moved[start:start + 1], right_t(gains[b] - eye), True)
        l = l + p_ref[b, 0]
        g = g + m_ref[spot[b]]
        e_ref[b, 0] = e
        l_ref[b, 0] = l
        g_ref[spot[b]] = g
        acc_e[b] = e
        acc_l[b] = l
        acc_g[b] = jnp.broadcast_to(g, (8, n))

    @pl.when(s == 0)
    def _():
        for b in range(blocks):
            finish(b, gains[b], jnp.zeros((n, n), F32), jnp.zeros((1, n), F32))

    @pl.when(s > 0)
    def _():
        for b in range(blocks):
            gl = left(gains[b] - eye)
            e = acc_e[b] + mm(gl, right(acc_e[b]))
            inner = acc_l[b] + mm(gl, right(acc_l[b]))
            finish(b, e, inner, acc_g[b][:1])

    @pl.when(s == length - 1)
    def _():
        parts = [(acc_e[b], acc_g[b][:1], acc_l[b]) for b in range(blocks)]
        while len(parts) > 1:
            parts = [compose(parts[i], parts[i + 1]) for i in range(0, len(parts), 2)]
        store(tot_ref, parts[0])


def exchange_kernel(sizes, t_ref, o_ref, tot, exc, got, s_sem, r_sem, s2_sem, r2_sem, s3_sem):
    n = t_ref.shape[1]
    tri, start, full = layout(n)
    grp, ta = lax.axis_index("grp"), lax.axis_index("ta")
    core = lax.rem(ta, 2)
    sib = (grp, ta + 1 - 2 * core)
    partners = []
    relay = -1
    for name, size in sizes:
        step = 1
        while step < size:
            pos = ta if name == "ta" else grp
            bit = lax.rem(lax.div(pos, step), 2)
            other = pos + step - 2 * step * bit
            if name == "ta" and step == 4:
                below = lax.rem(lax.div(pos, 2), 2)
                near = (grp, pos + 2 - 4 * below)
                edge = below != bit
                other = other + 2 - 4 * below
                relay = len(partners)
            partners.append(((grp, other) if name == "ta" else (other, ta), bit))
            step *= 2
    rounds = len(partners)
    barrier = pltpu.get_barrier_semaphore()
    for dev, _ in partners:
        pl.semaphore_signal(barrier, inc=1, device_id=dev, device_id_type=MESH)
    pl.semaphore_wait(barrier, rounds)

    def copy(src, dst, a, b, dev):
        return pltpu.make_async_remote_copy(
            src_ref=src, dst_ref=dst, send_sem=a, recv_sem=b, device_id=dev, device_id_type=MESH)

    def pick(c, x, y):
        return tuple(jnp.where(c, i, j) for i, j in zip(x, y))

    def extend(k):
        was_low = partners[k - 1][1] == 0
        if k == 1:
            eye = unit(n)
            store(exc.at[1], pick(was_low, load(got.at[0]), (eye, jnp.zeros((1, n), F32), jnp.zeros((n, n), F32))))
        else:
            mine = load(exc.at[(k - 1) % 2])
            store(exc.at[k % 2], pick(was_low, compose(mine, load(got.at[k - 1])), mine))

    def guard(k):
        return pl.when(edge) if k == relay else (lambda f: f())

    for k, (dev, bit) in enumerate(partners):
        final = k == rounds - 1
        low = bit == 0
        src = t_ref if k == 0 else tot.at[k]
        if k == 0:
            send = copy(src, got.at[k], s_sem.at[k, 0], r_sem.at[k, 0], dev)
            send.start()
            send.wait()
        else:
            size = (start if final else full) // 2
            count = 2 if final else 4
            each = size // count // 8 * 8
            sends, swaps, passes = [], [], []
            for c in range(count):
                length = each if c < count - 1 else size - each * (count - 1)
                rows = pl.ds(pl.multiple_of(core * size + c * each, 8), length)
                spot = got.at[k, rows]
                sends.append(copy(src.at[rows], spot, s_sem.at[k, c], r_sem.at[k, c], dev))
                swaps.append(copy(spot, spot, s2_sem.at[k, c], r2_sem.at[k, c], sib))
                if k == relay:
                    passes.append(copy(spot, spot, s3_sem.at[c], r_sem.at[k, c], near))

            @guard(k)
            def _():
                for send in sends:
                    send.start()

            if k != relay:
                extend(k)
            for c in range(count):
                sends[c].wait_recv()
                if k == relay:
                    pl.when(edge)(passes[c].start)
                swaps[c].start()
                if k == relay and c == 1:
                    extend(k)
            for swap in swaps:
                swap.wait()

            @guard(k)
            def _():
                for send in sends:
                    send.wait_send()
                for send in passes:
                    send.wait_send()
        if not final:
            mine, theirs = load(src), load(got.at[k])
            store(tot.at[k + 1], compose(pick(low, mine, theirs), pick(low, theirs, mine)))
    mine = load(exc.at[(rounds - 1) % 2])
    _, g, l = compose(mine, load(got.at[rounds - 1], False), want_e=False)
    o_ref[0:n] = jnp.where(low, l, mine[2])
    o_ref[n:n + PAD] = wide(jnp.where(low, g, mine[1]))


def apply_kernel(blocks, length, c_ref, e_ref, l_ref, g_ref, m_ref, o_ref, carry):
    n = e_ref.shape[-1]

    @pl.when(pl.program_id(0) == 0)
    def _():
        carry[...] = c_ref[...]

    cov, mean = right(carry[0:n]), carry[n:n + 8][:1]
    inner = mm(left(jnp.concatenate([e_ref[0, i] for i in range(length)], axis=0)), cov)
    for i in reversed(range(length)):
        e = e_ref[0, i]
        l, g = push(inner[i * n:(i + 1) * n], mean, right_t(e))
        l = l + l_ref[0, i]
        spot = pl.ds((blocks - 1 - pl.program_id(0)) * length + i, 1)
        g = g + g_ref[spot]
        o_ref[0, i] = l
        m_ref[spot] = g
    carry[0:n] = l
    carry[n:n + PAD] = wide(g)


def body(transition, filtered_mean, filtered_cov, pred_precision):
    steps, n = filtered_mean.shape
    blocks = 4
    length = steps // blocks
    half = n + PAD
    mat = (blocks, length, n, n)
    limit = 56 * 1024 * 1024
    flops = 2 * n * n * n * 3
    by_pos = lambda shape: pl.BlockSpec((blocks, 1) + shape, lambda s: (0, length - 1 - s, 0, 0))
    whole = lambda shape: pl.BlockSpec(shape, lambda s: (0,) * len(shape))
    e, l, g, total = pl.pallas_call(
        functools.partial(local_kernel, blocks, length),
        grid=(length,),
        in_specs=[whole((n, n)), whole((steps, n)), by_pos((n, n)), by_pos((n, n))],
        out_specs=[by_pos((n, n)), by_pos((n, n)), whole((steps, n)), whole((layout(n)[2], n))],
        out_shape=[
            jax.ShapeDtypeStruct(mat, F32),
            jax.ShapeDtypeStruct(mat, F32),
            jax.ShapeDtypeStruct((steps, n), F32),
            jax.ShapeDtypeStruct((layout(n)[2], n), F32),
        ],
        scratch_shapes=[
            pltpu.VMEM((blocks, n, n), F32),
            pltpu.VMEM((blocks, n, n), F32),
            pltpu.VMEM((blocks, 8, n), F32),
            pltpu.VMEM((3 * n, n), BF16),
        ],
        compiler_params=pltpu.CompilerParams(vmem_limit_bytes=limit),
        cost_estimate=pl.CostEstimate(flops=80 * flops, bytes_accessed=16 * steps * n * n, transcendentals=0),
    )(transition, filtered_mean, filtered_cov.reshape(mat), pred_precision.reshape(mat))

    sizes = (("ta", lax.axis_size("ta")), ("grp", lax.axis_size("grp")))
    rounds = sum(size.bit_length() - 1 for _, size in sizes)
    vmem = pl.BlockSpec(memory_space=pltpu.VMEM)
    carried = pl.pallas_call(
        functools.partial(exchange_kernel, sizes),
        in_specs=[vmem],
        out_specs=vmem,
        out_shape=jax.ShapeDtypeStruct((half, n), F32),
        scratch_shapes=[
            pltpu.VMEM((rounds, layout(n)[2], n), F32),
            pltpu.VMEM((2, layout(n)[2], n), F32),
            pltpu.VMEM((rounds, layout(n)[2], n), F32),
        ] + [pltpu.SemaphoreType.DMA((rounds, 4))] * 4 + [pltpu.SemaphoreType.DMA((4,))],
        compiler_params=pltpu.CompilerParams(
            vmem_limit_bytes=limit, collective_id=0, has_side_effects=True),
    )(total)

    back = lambda shape: pl.BlockSpec((1, length) + shape, lambda s: (blocks - 1 - s, 0, 0, 0))
    mean, cov = pl.pallas_call(
        functools.partial(apply_kernel, blocks, length),
        grid=(blocks,),
        in_specs=[whole((half, n)), back((n, n)), back((n, n)), whole((steps, n))],
        out_specs=[whole((steps, n)), back((n, n))],
        out_shape=[jax.ShapeDtypeStruct((steps, n), F32), jax.ShapeDtypeStruct(mat, F32)],
        scratch_shapes=[pltpu.VMEM((half, n), F32)],
        compiler_params=pltpu.CompilerParams(vmem_limit_bytes=limit),
    )(carried, e, l, g)
    return mean, cov.reshape(steps, n, n)


def solution(mesh):
    return jax.shard_map(
        body,
        mesh=mesh,
        in_specs=(
            P(),
            P(("grp", "ta"), None),
            P(("grp", "ta"), None, None),
            P(("grp", "ta"), None, None),
        ),
        out_specs=(P(("grp", "ta"), None), P(("grp", "ta"), None, None)),
        check_vma=False,
    )
```
